512 devices in a mesh: tm: 8 (over y, z_hi), space: 64 (over x, z_lo, core).
Axes of the slice: x: 4, y: 4, z: 16 (z_hi: 2, z_lo: 8; z = z_hi * 8 + z_lo), core: 2. Of those that a mesh axis runs over, the one named last changes fastest.
Arguments:
- forcing: float32 [32, 2, 64, 128, 128], P('tm', None, 'space'), may hold values from -6 to 6
- init_state: float32 [2, 64, 128, 128], P(None, 'space'), may hold values from -6 to 6
- prev_last: float32 [2, 64, 128, 128], P(None, 'space'), may hold values from -6 to 6
- diff_h: float32 [64, 128, 128], P('space'), may hold values from 0.04 to 0.24
- vel_x: float32 [64, 128, 128], P('space'), may hold values from -0.2 to 0.2
- vel_y: float32 [64, 128, 128], P('space'), may hold values from -0.2 to 0.2
- diff_z: float32 [64, 128, 128], P('space'), may hold values from 0.05 to 0.4
Outputs:
- iterate: float32 [32, 2, 64, 128, 128], P('tm', None, 'space')
The draws below stay inside these ranges and needn't reach their ends.
All inputs are finite; a program needn't handle non-finite values.
Results may differ from the reference program's by a relative error of at most 0.0003.
Values sent between devices are 32-bit elements; how exact they have to be, the bound alone decides.
No kernel may reach another device: no remote copies, remote signals or barrier semaphores. Data moves between devices by JAX's collectives and lax.ppermute only.
A program may use at most 64 MiB of HBM per device.

```python
import math
import jax
import jax.numpy as jnp
from jax import lax

NT = 32
TR = 2
NZ = 128
NY = 128
SWEEPS = 2
NX = 64


def block_levels(own_key, dims, split, smallest, high):
    level, own = 1.0, jax.random.fold_in(own_key, 6)
    for axis_at, parts in split:
        draws = jnp.exp(jax.random.uniform(jax.random.fold_in(own, axis_at), (parts,), jnp.float32, smallest / len(split), high / len(split)))
        level = level * jnp.repeat(draws, dims[axis_at] // parts).reshape([-1 if axis == axis_at else 1 for axis in range(len(dims))])
    return level


def noise(key, shape, width, limit, shards=(), held_as=jnp.bfloat16):
    result = width * jax.random.normal(key, shape, jnp.float32)
    if shards:
        result = result * block_levels(key, shape, shards, -0.22, 0.18)
    return jnp.clip(result, -limit, limit).astype(held_as)


def setup_inputs(seed: int = 0) -> dict:
    key_of = jax.random.split(jax.random.key(seed), 8)
    return {
        "forcing": noise(key_of[0], (NT, TR, NX, NY, NZ), 1.0, 6.0, ((0, 8), (2, 64)), jnp.float32),
        "init_state": noise(key_of[1], (TR, NX, NY, NZ), 1.0, 6.0, ((1, 64),), jnp.float32),
        "prev_last": noise(key_of[2], (TR, NX, NY, NZ), 1.0, 6.0, ((1, 64),), jnp.float32),
        "diff_h": jnp.clip(jnp.exp(math.log(0.24) - 1.7917595 * jax.random.uniform(key_of[3], (NX, NY, NZ), jnp.float32) ** block_levels(key_of[3], (NX, NY, NZ), ((0, 64),), -0.2, 0.2)), 0.04, 0.24),
        "vel_x": jnp.clip(jax.random.uniform(key_of[4], (NX, NY, NZ), jnp.float32, -0.2, 0.2) * block_levels(key_of[4], (NX, NY, NZ), ((0, 64),), -0.4, 0.0), -0.2, 0.2),
        "vel_y": jnp.clip(jax.random.uniform(key_of[5], (NX, NY, NZ), jnp.float32, -0.2, 0.2) * block_levels(key_of[5], (NX, NY, NZ), ((0, 64),), -0.4, 0.0), -0.2, 0.2),
        "diff_z": jnp.clip(jnp.exp(math.log(0.4) - 2.0794415 * jax.random.uniform(key_of[6], (NX, NY, NZ), jnp.float32) ** block_levels(key_of[6], (NX, NY, NZ), ((0, 64),), -0.2, 0.2)), 0.05, 0.4),
    }


corner_weight = 0.5


def phase_table(rows, cols, total):
    product = (rows[:, None] * cols[None, :]) % total
    return product.astype(jnp.float32) * (2.0 * math.pi / total)


def along_y(field, diff_h, vel_y):
    pads = [(0, 0)] * (field.ndim - 2) + [(1, 1), (0, 0)]
    padded = jnp.pad(field, pads)
    return field + (diff_h + vel_y) * padded[..., :-2, :] - 2.0 * diff_h * field + (diff_h - vel_y) * padded[..., 2:, :]


def along_z(field, diff_z):
    pads = [(0, 0)] * (field.ndim - 1) + [(1, 1)]
    padded = jnp.pad(field, pads)
    return diff_z * (padded[..., :-2] - 2.0 * field + padded[..., 2:])


def along_x(center, left, right, diff_h, vel_x):
    return center + (diff_h + vel_x) * left - 2.0 * diff_h * center + (diff_h - vel_x) * right


def operate(field, diff_h, vel_x, vel_y, diff_z):
    smoothed = along_y(field, diff_h, vel_y)
    pads = [(0, 0)] * (field.ndim - 3) + [(1, 1), (0, 0), (0, 0)]
    padded = jnp.pad(smoothed, pads)
    mixed = along_x(smoothed, padded[..., :-2, :, :], padded[..., 2:, :, :], diff_h, vel_x)
    return mixed - field + along_z(field, diff_z)


def reference(forcing, init_state, prev_last, diff_h, vel_x, vel_y, diff_z):
    shape = forcing.shape
    steps = jnp.arange(NT, dtype=jnp.int32)
    steps_f = steps.astype(jnp.float32)
    rhs = forcing.at[0].add(init_state - corner_weight * prev_last)
    power = jnp.exp(steps_f * (math.log(corner_weight) / NT))
    scaled = rhs * power[:, None, None, None, None]
    table = phase_table(steps, steps, NT)
    cosines = jnp.cos(table)
    sines = jnp.sin(table)
    flat = scaled.reshape(NT, -1)
    spec_re = jnp.dot(cosines, flat, precision=lax.Precision.HIGHEST).reshape(shape)
    spec_im = -jnp.dot(sines, flat, precision=lax.Precision.HIGHEST).reshape(shape)
    ratio = jnp.exp(jnp.float32(math.log(corner_weight) / NT))
    theta = steps_f * (2.0 * math.pi / NT)
    lam_re = 1.0 - ratio * jnp.cos(theta)
    lam_im = ratio * jnp.sin(theta)
    shift = 1.0 - (1.0 - 2.0 * diff_h) * (1.0 - 2.0 * diff_h) + 2.0 * diff_z

    def solve_one(items):
        wr, wi, lr, li = items
        dr = lr + shift
        di = li
        denom = dr * dr + di * di
        yr = (wr * dr + wi * di) / denom
        yi = (wi * dr - wr * di) / denom
        for sweep in range(SWEEPS):
            kr = operate(yr, diff_h, vel_x, vel_y, diff_z)
            ki = operate(yi, diff_h, vel_x, vel_y, diff_z)
            mr = lr * yr - li * yi - kr
            mi = lr * yi + li * yr - ki
            rr = wr - mr
            ri = wi - mi
            yr = yr + (rr * dr + ri * di) / denom
            yi = yi + (ri * dr - rr * di) / denom
        return yr, yi

    solved_re, solved_im = lax.map(solve_one, (spec_re, spec_im, lam_re, lam_im))
    back = jnp.exp(steps_f * (-math.log(corner_weight) / NT)) / NT
    total = jnp.dot(cosines, solved_re.reshape(NT, -1), precision=lax.Precision.HIGHEST) - jnp.dot(sines, solved_im.reshape(NT, -1), precision=lax.Precision.HIGHEST)
    return (total * back[:, None]).reshape(shape)
```

```python
import math

import jax
import jax.numpy as jnp
from jax import lax
from jax.experimental import pallas as pl
from jax.experimental.pallas import tpu as pltpu
from jax.sharding import PartitionSpec as P

CORNER = 0.5
NT = 32
LOG_G = math.log(CORNER) / NT
G = math.exp(LOG_G)
ROWS = 32
WIDE = ROWS + 4
SMOOTH = ROWS + 2
VMEM = 24 * 1024 * 1024

CHIPS_X, CHIPS_Y, CHIPS_Z, CORES = 4, 4, 16, 2


def flat_index(x, y, z, core):
    half = CHIPS_Z // 2
    return (y * 2 + z // half) * (CHIPS_X * half * CORES) + (x * half + z % half) * CORES + core


def x_neighbours():
    pairs = []
    half = CHIPS_Z // 2
    for x in range(CHIPS_X):
        for y in range(CHIPS_Y):
            for z in range(CHIPS_Z):
                here = flat_index(x, y, z, 0)
                pairs.append((here, flat_index(x, y, z, 1)))
                step = x + 1 if z % half == half - 1 else x
                if step < CHIPS_X:
                    pairs.append((flat_index(x, y, z, 1), flat_index(step, y, (z + 1) % CHIPS_Z, 0)))
    return pairs


def real_fft(values):
    n = len(values)
    if n == 1:
        return [(values[0], None)]
    if n == 2:
        return [(values[0] + values[1], None), (values[0] - values[1], None)]
    even, odd = real_fft(values[0::2]), real_fft(values[1::2])
    out = [None] * (n // 2 + 1)
    out[0] = (even[0][0] + odd[0][0], None)
    out[n // 2] = (even[0][0] - odd[0][0], None)
    for k in range(1, n // 4):
        c, s = math.cos(2 * math.pi * k / n), math.sin(2 * math.pi * k / n)
        er, ei = even[k]
        orr, oi = odd[k]
        tr = c * orr + s * oi
        ti = c * oi - s * orr
        out[k] = (er + tr, ei + ti)
        out[n // 2 - k] = (er - tr, ti - ei)
    out[n // 4] = (even[n // 4][0], -odd[n // 4][0])
    return out


def real_ifft(spec):
    n = 2 * (len(spec) - 1)
    if n == 2:
        return [spec[0][0] + spec[1][0], spec[0][0] - spec[1][0]]
    even, odd = [None] * (n // 4 + 1), [None] * (n // 4 + 1)
    even[0] = (spec[0][0] + spec[n // 2][0], None)
    odd[0] = (spec[0][0] - spec[n // 2][0], None)
    for k in range(1, n // 4):
        c, s = math.cos(2 * math.pi * k / n), math.sin(2 * math.pi * k / n)
        ar, ai = spec[k]
        br, bi = spec[n // 2 - k]
        even[k] = (ar + br, ai - bi)
        dr, di = ar - br, ai + bi
        odd[k] = (c * dr - s * di, c * di + s * dr)
    even[n // 4] = (2.0 * spec[n // 4][0], None)
    odd[n // 4] = (-2.0 * spec[n // 4][1], None)
    first, second = real_ifft(even), real_ifft(odd)
    out = [None] * n
    out[0::2], out[1::2] = first, second
    return out


def inverses(pair, h):
    if pair == 0:
        return 1.0 / (h + (1.0 - G)), 1.0 / (h + (1.0 + G))
    theta = 2.0 * math.pi * pair / NT
    real = h + (1.0 - G * math.cos(theta))
    imag = G * math.sin(theta)
    scale = 1.0 / (real * real + imag * imag)
    return real * scale, imag * scale


def apply_inverse(pair, inv, first, second):
    if pair == 0:
        return first * inv[0], second * inv[1]
    return first * inv[0] + second * inv[1], second * inv[0] - first * inv[1]


def pack_kernel(ids, forcing, init, prev, diff_h, vel_x, vel_y, diff_z, blocks, coeffs):
    quarter, odd_x = ids[0], ids[1]
    first = (ids[2] == 0).astype(jnp.float32)
    for half in range(2):
        tracer = odd_x if half == 0 else 1 - odd_x
        for part in range(4):
            dest = 2 * part + half
            low, high = max(ROWS * part - 2, 0), min(ROWS * part + ROWS + 2, 128)
            skip = low - (ROWS * part - 2)
            for step in range(4):
                value = forcing[step, tracer, low:high, :]
                if step == 0:
                    value = value + first * (init[tracer, low:high, :] - CORNER * prev[tracer, low:high, :])
                base = WIDE * step
                blocks[dest, base + skip : base + skip + high - low, :] = value
                if skip:
                    blocks[dest, base : base + skip, :] = jnp.zeros((skip, 128), jnp.float32)
                rest = WIDE - skip - (high - low)
                if rest:
                    blocks[dest, base + WIDE - rest : base + WIDE, :] = jnp.zeros((rest, 128), jnp.float32)
    for part in range(4):

        @pl.when(quarter == part)
        def _():
            low, high = max(ROWS * part - 2, 0), min(ROWS * part + ROWS + 2, 128)
            skip = low - (ROWS * part - 2)
            if part in (0, 3):
                coeffs[...] = jnp.zeros(coeffs.shape, jnp.float32)
            for i, ref in enumerate((diff_h, vel_x, vel_y, diff_z)):
                coeffs[i, skip : skip + high - low, :] = ref[low:high, :]


def chunks(start, count):
    out = list(range(start, start + count - 7, 8))
    if count % 8:
        out.append(start + count - 8)
    return out


def smooth_rows(coeffs, field, start, index):
    d = coeffs[0, start : start + 8, :]
    vy = coeffs[2, start : start + 8, :]
    return (
        (1.0 - 2.0 * d) * field[index, start : start + 8, :]
        + (d + vy) * field[index, start - 1 : start + 7, :]
        + (d - vy) * field[index, start + 1 : start + 9, :]
    )


def shift_of(d, dz):
    a = 1.0 - 2.0 * d
    return 1.0 - a * a + 2.0 * dz


def first_kernel(gathered, coeffs, start_field, smoothed):
    for r in chunks(0, WIDE):
        values = []
        for n in range(NT):
            base = WIDE * (n % 4) + r
            value = gathered[n // 4, base : base + 8, :]
            values.append(value * math.exp(n * LOG_G) if n else value)
        spec = real_fft(values)
        h = shift_of(coeffs[0, r : r + 8, :], coeffs[3, r : r + 8, :])
        for pair in range(16):
            a, b = (spec[0][0], spec[16][0]) if pair == 0 else spec[pair]
            ya, yb = apply_inverse(pair, inverses(pair, h), a, b)
            start_field[2 * pair, r : r + 8, :] = ya
            start_field[2 * pair + 1, r : r + 8, :] = yb
    for r in chunks(1, SMOOTH):
        for f in range(NT):
            base = SMOOTH * f + r - 1
            smoothed[base : base + 8, :] = smooth_rows(coeffs, start_field, r, f)


def sweep_rows(coeffs, field, left, right, start, bases, keep):
    rows = slice(start, start + 8)
    d, vx, vy, dz = (coeffs[i, rows, :] for i in range(4))
    a = 1.0 - 2.0 * d
    up, down = a * (d + vy), a * (d - vy)
    west, east = d + vx, d - vx
    h = shift_of(d, dz)
    lane = lax.broadcasted_iota(jnp.int32, (8, 128), 1)
    below = jnp.where(lane == 0, 0.0, dz)
    above = jnp.where(lane == 127, 0.0, dz)
    for pair in range(16):
        both = []
        for f in (2 * pair, 2 * pair + 1):
            center = field[f, rows, :]
            base = bases(f)
            both.append(
                up * field[f, start - 1 : start + 7, :]
                + down * field[f, start + 1 : start + 9, :]
                + west * left[base : base + 8, :]
                + east * right[base : base + 8, :]
                + below * pltpu.roll(center, 1, 1)
                + above * pltpu.roll(center, 127, 1)
            )
        keep(pair, *apply_inverse(pair, inverses(pair, h), *both))


def second_kernel(coeffs, start_field, left, right, next_field, smoothed):
    for r in chunks(1, SMOOTH):

        def keep(pair, a, b):
            for f, value in ((2 * pair, a), (2 * pair + 1, b)):
                next_field[f, r : r + 8, :] = start_field[f, r : r + 8, :] + value

        sweep_rows(coeffs, start_field, left, right, r, lambda f: SMOOTH * f + r - 1, keep)
    for r in chunks(2, ROWS):
        for f in range(NT):
            base = ROWS * f + r - 2
            smoothed[base : base + 8, :] = smooth_rows(coeffs, next_field, r, f)


def third_kernel(coeffs, start_field, next_field, left, right, blocks):
    for r in chunks(2, ROWS):
        spec = [None] * 17

        def keep(pair, a, b):
            a = start_field[2 * pair, r : r + 8, :] + a
            b = start_field[2 * pair + 1, r : r + 8, :] + b
            if pair == 0:
                spec[0], spec[16] = (a, None), (b, None)
            else:
                spec[pair] = (a, b)

        sweep_rows(coeffs, next_field, left, right, r, lambda f: ROWS * f + r - 2, keep)
        for n, value in enumerate(real_ifft(spec)):
            base = ROWS * (n % 4) + r - 2
            blocks[n // 4, base : base + 8, :] = value * (math.exp(-n * LOG_G) / NT)


def unpack_kernel(ids, blocks, out):
    odd_x = ids[1]
    for half in range(2):
        tracer = odd_x if half == 0 else 1 - odd_x
        for part in range(4):
            for step in range(4):
                out[step, tracer, ROWS * part : ROWS * part + ROWS, :] = blocks[
                    2 * part + half, ROWS * step : ROWS * step + ROWS, :
                ]


def f32(*shape):
    return jax.ShapeDtypeStruct(shape, jnp.float32)


def call(kernel, outs, scalars=0, inputs=1):
    vmem = pl.BlockSpec(memory_space=pltpu.VMEM)
    smem = pl.BlockSpec(memory_space=pltpu.SMEM)
    many = isinstance(outs, tuple)
    return pl.pallas_call(
        kernel,
        out_shape=outs,
        in_specs=[smem] * scalars + [vmem] * inputs,
        out_specs=(vmem,) * len(outs) if many else vmem,
        compiler_params=pltpu.CompilerParams(vmem_limit_bytes=VMEM),
    )


def shards(forcing, init_state, prev_last, diff_h, vel_x, vel_y, diff_z):
    pairs = x_neighbours()
    back = [(b, a) for a, b in pairs]
    axes = ("tm", "space")
    group, place = lax.axis_index("tm"), lax.axis_index("space")
    ids = jnp.stack([group // 2, (place // 16) % 2, group]).astype(jnp.int32)

    blocks, coeffs = call(pack_kernel, (f32(8, 4 * WIDE, 128), f32(4, 40, 128)), 1, 7)(
        ids,
        forcing.reshape(4, 2, 128, 128),
        init_state.reshape(2, 128, 128),
        prev_last.reshape(2, 128, 128),
        *(c.reshape(128, 128) for c in (diff_h, vel_x, vel_y, diff_z)),
    )
    gathered = lax.all_to_all(blocks, "tm", 0, 0)
    start_field, smoothed = call(first_kernel, (f32(NT, 40, 128), f32(NT * SMOOTH, 128)), 0, 2)(gathered, coeffs)
    left = lax.ppermute(smoothed, axes, pairs)
    right = lax.ppermute(smoothed, axes, back)
    next_field, smoothed = call(second_kernel, (f32(NT, 40, 128), f32(NT * ROWS, 128)), 0, 4)(
        coeffs, start_field, left, right
    )
    left = lax.ppermute(smoothed, axes, pairs)
    right = lax.ppermute(smoothed, axes, back)
    blocks = call(third_kernel, f32(8, 4 * ROWS, 128), 0, 5)(coeffs, start_field, next_field, left, right)
    gathered = lax.all_to_all(blocks, "tm", 0, 0)
    out = call(unpack_kernel, f32(4, 2, 128, 128), 1, 1)(ids, gathered)
    return out.reshape(forcing.shape)


def solution(mesh):
    return jax.shard_map(
        shards,
        mesh=mesh,
        in_specs=(
            P("tm", None, "space", None, None),
            P(None, "space", None, None),
            P(None, "space", None, None),
            P("space", None, None),
            P("space", None, None),
            P("space", None, None),
            P("space", None, None),
        ),
        out_specs=P("tm", None, "space", None, None),
        check_vma=False,
    )
```

```python
import math

import jax
import jax.numpy as jnp
from jax import lax
from jax.experimental import pallas as pl
from jax.experimental.pallas import tpu as pltpu
from jax.sharding import PartitionSpec as P

CORNER = 0.5
NT = 32
LOG_G = math.log(CORNER) / NT
G = math.exp(LOG_G)
ROWS = 32
WIDE = ROWS + 4
SMOOTH = ROWS + 2
VMEM = 24 * 1024 * 1024

CHIPS_X, CHIPS_Y, CHIPS_Z, CORES = 4, 4, 16, 2


def flat_index(x, y, z, core):
    half = CHIPS_Z // 2
    return (y * 2 + z // half) * (CHIPS_X * half * CORES) + (x * half + z % half) * CORES + core


def position():
    group, place = lax.axis_index("tm"), lax.axis_index("space")
    return group >> 1, group & 1, (place >> 4) & 1, place & 1


def swaps():
    near, far = [], []
    half = CHIPS_Z // 2
    for x in range(CHIPS_X):
        for y in range(CHIPS_Y):
            for z in range(CHIPS_Z):
                here, mate = flat_index(x, y, z, 0), flat_index(x, y, z, 1)
                near += [(here, mate), (mate, here)]
                step = x + 1 if z % half == half - 1 else x
                if step < CHIPS_X:
                    after = flat_index(step, y, (z + 1) % CHIPS_Z, 0)
                    far += [(mate, after), (after, mate)]
    return near, far


def real_fft(values):
    n = len(values)
    if n == 1:
        return [(values[0], None)]
    if n == 2:
        return [(values[0] + values[1], None), (values[0] - values[1], None)]
    even, odd = real_fft(values[0::2]), real_fft(values[1::2])
    out = [None] * (n // 2 + 1)
    out[0] = (even[0][0] + odd[0][0], None)
    out[n // 2] = (even[0][0] - odd[0][0], None)
    for k in range(1, n // 4):
        c, s = math.cos(2 * math.pi * k / n), math.sin(2 * math.pi * k / n)
        er, ei = even[k]
        orr, oi = odd[k]
        tr = c * orr + s * oi
        ti = c * oi - s * orr
        out[k] = (er + tr, ei + ti)
        out[n // 2 - k] = (er - tr, ti - ei)
    out[n // 4] = (even[n // 4][0], -odd[n // 4][0])
    return out


def real_ifft(spec):
    n = 2 * (len(spec) - 1)
    if n == 2:
        return [spec[0][0] + spec[1][0], spec[0][0] - spec[1][0]]
    even, odd = [None] * (n // 4 + 1), [None] * (n // 4 + 1)
    even[0] = (spec[0][0] + spec[n // 2][0], None)
    odd[0] = (spec[0][0] - spec[n // 2][0], None)
    for k in range(1, n // 4):
        c, s = math.cos(2 * math.pi * k / n), math.sin(2 * math.pi * k / n)
        ar, ai = spec[k]
        br, bi = spec[n // 2 - k]
        even[k] = (ar + br, ai - bi)
        dr, di = ar - br, ai + bi
        odd[k] = (c * dr - s * di, c * di + s * dr)
    even[n // 4] = (2.0 * spec[n // 4][0], None)
    odd[n // 4] = (-2.0 * spec[n // 4][1], None)
    first, second = real_ifft(even), real_ifft(odd)
    out = [None] * n
    out[0::2], out[1::2] = first, second
    return out


def inverses(pair, h):
    if pair == 0:
        return 1.0 / (h + (1.0 - G)), 1.0 / (h + (1.0 + G))
    theta = 2.0 * math.pi * pair / NT
    real = h + (1.0 - G * math.cos(theta))
    imag = G * math.sin(theta)
    scale = 1.0 / (real * real + imag * imag)
    return real * scale, imag * scale


def apply_inverse(pair, inv, first, second):
    if pair == 0:
        return first * inv[0], second * inv[1]
    return first * inv[0] + second * inv[1], second * inv[0] - first * inv[1]


def window(part):
    low, high = max(ROWS * part - 2, 0), min(ROWS * part + ROWS + 2, 128)
    return low, high, low - (ROWS * part - 2)


def pack_kernel(forcing, init, prev, *refs):
    sources, (blocks, coeffs), held, sems = refs[:4], refs[4:6], refs[6:13], refs[13]
    quarter, own_half, odd_x, _ = position()
    steps, values, firsts = held[0], held[1:5], held[5:7]
    loads = [pltpu.make_async_copy(forcing.at[step], steps.at[step], sems.at[step]) for step in range(4)]
    others = [pltpu.make_async_copy(source, values[i], sems.at[4 + i]) for i, source in enumerate(sources)]
    holds_first = jnp.logical_and(quarter == 0, own_half == 0)
    for copy in loads + others:
        copy.start()

    @pl.when(holds_first)
    def _():
        pair = [pltpu.make_async_copy(a, firsts[i], sems.at[8 + i]) for i, a in enumerate((init, prev))]
        for copy in pair:
            copy.start()
        for copy in pair:
            copy.wait()

    loads[0].wait()

    @pl.when(holds_first)
    def _():
        steps[0] += firsts[0][...] - CORNER * firsts[1][...]

    for step in range(4):
        if step:
            loads[step].wait()
        for half in range(2):
            tracer = odd_x if half == 0 else 1 - odd_x
            for part in range(4):
                low, high, skip = window(part)
                rest = WIDE - skip - (high - low)
                dest, base = 2 * part + half, WIDE * step
                blocks[dest, base + skip : base + skip + high - low, :] = steps[step, tracer, low:high, :]
                if skip:
                    blocks[dest, base : base + skip, :] = jnp.zeros((skip, 128), jnp.float32)
                if rest:
                    blocks[dest, base + WIDE - rest : base + WIDE, :] = jnp.zeros((rest, 128), jnp.float32)
    for copy in others:
        copy.wait()
    for part in range(4):

        @pl.when(quarter == part)
        def _():
            low, high, skip = window(part)
            if part in (0, 3):
                coeffs[...] = jnp.zeros(coeffs.shape, jnp.float32)
            for i, ref in enumerate(values):
                coeffs[i, skip : skip + high - low, :] = ref[low:high, :]


def chunks(start, count):
    out = list(range(start, start + count - 7, 8))
    if count % 8:
        out.append(start + count - 8)
    return out


def smooth_rows(coeffs, field, start, index):
    d = coeffs[0, start : start + 8, :]
    vy = coeffs[2, start : start + 8, :]
    return (
        (1.0 - 2.0 * d) * field[index, start : start + 8, :]
        + (d + vy) * field[index, start - 1 : start + 7, :]
        + (d - vy) * field[index, start + 1 : start + 9, :]
    )


def shift_of(d, dz):
    a = 1.0 - 2.0 * d
    return 1.0 - a * a + 2.0 * dz


def first_kernel(gathered, coeffs, start_field, smoothed):
    for r in chunks(0, WIDE):
        values = []
        for n in range(NT):
            base = WIDE * (n % 4) + r
            value = gathered[n // 4, base : base + 8, :]
            values.append(value * math.exp(n * LOG_G) if n else value)
        spec = real_fft(values)
        h = shift_of(coeffs[0, r : r + 8, :], coeffs[3, r : r + 8, :])
        for pair in range(16):
            a, b = (spec[0][0], spec[16][0]) if pair == 0 else spec[pair]
            ya, yb = apply_inverse(pair, inverses(pair, h), a, b)
            start_field[2 * pair, r : r + 8, :] = ya
            start_field[2 * pair + 1, r : r + 8, :] = yb
    for r in chunks(1, SMOOTH):
        for f in range(NT):
            base = SMOOTH * f + r - 1
            smoothed[base : base + 8, :] = smooth_rows(coeffs, start_field, r, f)


def sweep_rows(coeffs, field, near, far, start, bases, keep):
    rows = slice(start, start + 8)
    d, vx, vy, dz = (coeffs[i, rows, :] for i in range(4))
    a = 1.0 - 2.0 * d
    up, down = a * (d + vy), a * (d - vy)
    sign = (2 * position()[3] - 1).astype(jnp.float32)
    beside, across = d + sign * vx, d - sign * vx
    h = shift_of(d, dz)
    lane = lax.broadcasted_iota(jnp.int32, (8, 128), 1)
    below = jnp.where(lane == 0, 0.0, dz)
    above = jnp.where(lane == 127, 0.0, dz)
    for pair in range(16):
        both = []
        for f in (2 * pair, 2 * pair + 1):
            center = field[f, rows, :]
            base = bases(f)
            both.append(
                up * field[f, start - 1 : start + 7, :]
                + down * field[f, start + 1 : start + 9, :]
                + beside * near[base : base + 8, :]
                + across * far[base : base + 8, :]
                + below * pltpu.roll(center, 1, 1)
                + above * pltpu.roll(center, 127, 1)
            )
        keep(pair, *apply_inverse(pair, inverses(pair, h), *both))


def second_kernel(coeffs, start_field, near, far, next_field, smoothed):
    for r in chunks(1, SMOOTH):

        def keep(pair, a, b):
            for f, value in ((2 * pair, a), (2 * pair + 1, b)):
                next_field[f, r : r + 8, :] = start_field[f, r : r + 8, :] + value

        sweep_rows(coeffs, start_field, near, far, r, lambda f: SMOOTH * f + r - 1, keep)
    for r in chunks(2, ROWS):
        for f in range(NT):
            base = ROWS * f + r - 2
            smoothed[base : base + 8, :] = smooth_rows(coeffs, next_field, r, f)


def third_kernel(coeffs, start_field, next_field, near, far, blocks):
    for r in chunks(2, ROWS):
        spec = [None] * 17

        def keep(pair, a, b):
            a = start_field[2 * pair, r : r + 8, :] + a
            b = start_field[2 * pair + 1, r : r + 8, :] + b
            if pair == 0:
                spec[0], spec[16] = (a, None), (b, None)
            else:
                spec[pair] = (a, b)

        sweep_rows(coeffs, next_field, near, far, r, lambda f: ROWS * f + r - 2, keep)
        for n, value in enumerate(real_ifft(spec)):
            base = ROWS * (n % 4) + r - 2
            blocks[n // 4, base : base + 8, :] = value * (math.exp(-n * LOG_G) / NT)


def unpack_kernel(gathered, out, sems):
    odd_x = position()[2]
    copies = []
    for half in range(2):
        tracer = odd_x if half == 0 else 1 - odd_x
        for part in range(4):
            block = 2 * part + half
            target = out.at[:, tracer, pl.ds(ROWS * part, ROWS), :]
            copies.append(pltpu.make_async_copy(gathered.at[block], target, sems.at[block]))
    for copy in copies:
        copy.start()
    for copy in copies:
        copy.wait()


def f32(*shape):
    return jax.ShapeDtypeStruct(shape, jnp.float32)


def call(kernel, outs, inputs=1, far_in=False, far_out=False, scratch=()):
    vmem = pl.BlockSpec(memory_space=pltpu.VMEM)
    hbm = pl.BlockSpec(memory_space=pltpu.HBM)
    out_spec = hbm if far_out else vmem
    return pl.pallas_call(
        kernel,
        out_shape=outs,
        in_specs=[hbm if far_in else vmem] * inputs,
        out_specs=(out_spec,) * len(outs) if isinstance(outs, tuple) else out_spec,
        scratch_shapes=list(scratch),
        compiler_params=pltpu.CompilerParams(vmem_limit_bytes=VMEM),
    )


def shards(forcing, init_state, prev_last, diff_h, vel_x, vel_y, diff_z):
    near, far = swaps()
    axes = ("tm", "space")
    operands = (
        forcing.reshape(4, 2, 128, 128),
        init_state.reshape(2, 128, 128),
        prev_last.reshape(2, 128, 128),
        *(c.reshape(128, 128) for c in (diff_h, vel_x, vel_y, diff_z)),
    )
    order = (0, 3, 4, 5, 6, 1, 2)
    scratch = [pltpu.VMEM(operands[i].shape, jnp.float32) for i in order] + [pltpu.SemaphoreType.DMA((10,))]
    blocks, coeffs = call(pack_kernel, (f32(8, 4 * WIDE, 128), f32(4, 40, 128)), 7, far_in=True, scratch=scratch)(
        *(pltpu.with_memory_space_constraint(a, pltpu.HBM) for a in operands)
    )
    gathered = lax.all_to_all(blocks, "tm", 0, 0)
    start_field, smoothed = call(first_kernel, (f32(NT, 40, 128), f32(NT * SMOOTH, 128)), 2)(gathered, coeffs)
    across = lax.ppermute(smoothed, axes, far)
    beside = lax.ppermute(smoothed, axes, near)
    next_field, smoothed = call(second_kernel, (f32(NT, 40, 128), f32(NT * ROWS, 128)), 4)(
        coeffs, start_field, beside, across
    )
    across = lax.ppermute(smoothed, axes, far)
    beside = lax.ppermute(smoothed, axes, near)
    blocks = call(third_kernel, f32(8, 4 * ROWS, 128), 5)(coeffs, start_field, next_field, beside, across)
    gathered = lax.all_to_all(blocks, "tm", 0, 0).reshape(8, 4, ROWS, 128)
    out = call(unpack_kernel, f32(4, 2, 128, 128), 1, far_out=True, scratch=[pltpu.SemaphoreType.DMA((8,))])(gathered)
    return out.reshape(forcing.shape)


def solution(mesh):
    return jax.shard_map(
        shards,
        mesh=mesh,
        in_specs=(
            P("tm", None, "space", None, None),
            P(None, "space", None, None),
            P(None, "space", None, None),
            P("space", None, None),
            P("space", None, None),
            P("space", None, None),
            P("space", None, None),
        ),
        out_specs=P("tm", None, "space", None, None),
        check_vma=False,
    )
```

```python
import math

import jax
import jax.numpy as jnp
from jax import lax
from jax.experimental import pallas as pl
from jax.experimental.pallas import tpu as pltpu
from jax.sharding import PartitionSpec as P

CORNER = 0.5
NT = 32
LOG_G = math.log(CORNER) / NT
G = math.exp(LOG_G)
ROWS = 32
WIDE = ROWS + 4
SMOOTH = ROWS + 2
VMEM = 24 * 1024 * 1024

CHIPS_X, CHIPS_Y, CHIPS_Z, CORES = 4, 4, 16, 2


def flat_index(x, y, z, core):
    half = CHIPS_Z // 2
    return (y * 2 + z // half) * (CHIPS_X * half * CORES) + (x * half + z % half) * CORES + core


def position():
    group, place = lax.axis_index("tm"), lax.axis_index("space")
    return group >> 1, group & 1, (place >> 4) & 1, place & 1, (place >> 1) & 7


THERE = (16449171, 477046, 13642849, 7670213, 9222671, 4329752, 11130092, 4187066)
BACK = (12686257, 15687872, 4709462, 3586597, 10243739, 11053039, 7473418, 1668476)


def slots_at(places, z):
    return [(place >> (3 * z)) & 7 for place in places]


def exchange(places, blocks):
    half = CHIPS_Z // 2
    groups = []
    for x in range(CHIPS_X):
        for z in range(half):
            slots = slots_at(places, z)
            for core in range(CORES):
                members = [0] * 8
                for group, slot in enumerate(slots):
                    members[slot] = flat_index(x, group // 2, z + half * (group % 2), core)
                groups.append(members)
    return lax.all_to_all(blocks, ("tm", "space"), 0, 0, axis_index_groups=groups)


def swaps():
    near, far = [], []
    half = CHIPS_Z // 2
    for x in range(CHIPS_X):
        for y in range(CHIPS_Y):
            for z in range(CHIPS_Z):
                here, mate = flat_index(x, y, z, 0), flat_index(x, y, z, 1)
                near += [(here, mate), (mate, here)]
                step = x + 1 if z % half == half - 1 else x
                if step < CHIPS_X:
                    after = flat_index(step, y, (z + 1) % CHIPS_Z, 0)
                    far += [(mate, after), (after, mate)]
    return near, far


def real_fft(values):
    n = len(values)
    if n == 1:
        return [(values[0], None)]
    if n == 2:
        return [(values[0] + values[1], None), (values[0] - values[1], None)]
    even, odd = real_fft(values[0::2]), real_fft(values[1::2])
    out = [None] * (n // 2 + 1)
    out[0] = (even[0][0] + odd[0][0], None)
    out[n // 2] = (even[0][0] - odd[0][0], None)
    for k in range(1, n // 4):
        c, s = math.cos(2 * math.pi * k / n), math.sin(2 * math.pi * k / n)
        er, ei = even[k]
        orr, oi = odd[k]
        tr = c * orr + s * oi
        ti = c * oi - s * orr
        out[k] = (er + tr, ei + ti)
        out[n // 2 - k] = (er - tr, ti - ei)
    out[n // 4] = (even[n // 4][0], -odd[n // 4][0])
    return out


def real_ifft(spec):
    n = 2 * (len(spec) - 1)
    if n == 2:
        return [spec[0][0] + spec[1][0], spec[0][0] - spec[1][0]]
    even, odd = [None] * (n // 4 + 1), [None] * (n // 4 + 1)
    even[0] = (spec[0][0] + spec[n // 2][0], None)
    odd[0] = (spec[0][0] - spec[n // 2][0], None)
    for k in range(1, n // 4):
        c, s = math.cos(2 * math.pi * k / n), math.sin(2 * math.pi * k / n)
        ar, ai = spec[k]
        br, bi = spec[n // 2 - k]
        even[k] = (ar + br, ai - bi)
        dr, di = ar - br, ai + bi
        odd[k] = (c * dr - s * di, c * di + s * dr)
    even[n // 4] = (2.0 * spec[n // 4][0], None)
    odd[n // 4] = (-2.0 * spec[n // 4][1], None)
    first, second = real_ifft(even), real_ifft(odd)
    out = [None] * n
    out[0::2], out[1::2] = first, second
    return out


def inverses(pair, h):
    if pair == 0:
        return 1.0 / (h + (1.0 - G)), 1.0 / (h + (1.0 + G))
    theta = 2.0 * math.pi * pair / NT
    real = h + (1.0 - G * math.cos(theta))
    imag = G * math.sin(theta)
    scale = 1.0 / (real * real + imag * imag)
    return real * scale, imag * scale


def apply_inverse(pair, inv, first, second):
    if pair == 0:
        return first * inv[0], second * inv[1]
    return first * inv[0] + second * inv[1], second * inv[0] - first * inv[1]


def window(part):
    low, high = max(ROWS * part - 2, 0), min(ROWS * part + ROWS + 2, 128)
    return low, high, low - (ROWS * part - 2)


def pack_kernel(forcing, init, prev, *refs):
    sources, (blocks, coeffs), held, sems = refs[:4], refs[4:6], refs[6:13], refs[13]
    quarter, own_half, odd_x, _, z = position()
    slots = slots_at(THERE, z)
    steps, values, firsts = held[0], held[1:5], held[5:7]
    loads = [pltpu.make_async_copy(forcing.at[step], steps.at[step], sems.at[step]) for step in range(4)]
    others = [pltpu.make_async_copy(source, values[i], sems.at[4 + i]) for i, source in enumerate(sources)]
    holds_first = jnp.logical_and(quarter == 0, own_half == 0)
    for copy in loads + others:
        copy.start()

    @pl.when(holds_first)
    def _():
        pair = [pltpu.make_async_copy(a, firsts[i], sems.at[8 + i]) for i, a in enumerate((init, prev))]
        for copy in pair:
            copy.start()
        for copy in pair:
            copy.wait()

    loads[0].wait()

    @pl.when(holds_first)
    def _():
        steps[0] += firsts[0][...] - CORNER * firsts[1][...]

    for step in range(4):
        if step:
            loads[step].wait()
        for half in range(2):
            tracer = odd_x if half == 0 else 1 - odd_x
            for part in range(4):
                low, high, skip = window(part)
                rest = WIDE - skip - (high - low)
                dest, base = slots[2 * part + half], WIDE * step
                blocks[dest, base + skip : base + skip + high - low, :] = steps[step, tracer, low:high, :]
                if skip:
                    blocks[dest, base : base + skip, :] = jnp.zeros((skip, 128), jnp.float32)
                if rest:
                    blocks[dest, base + WIDE - rest : base + WIDE, :] = jnp.zeros((rest, 128), jnp.float32)
    for copy in others:
        copy.wait()
    for part in range(4):

        @pl.when(quarter == part)
        def _():
            low, high, skip = window(part)
            if part in (0, 3):
                coeffs[...] = jnp.zeros(coeffs.shape, jnp.float32)
            for i, ref in enumerate(values):
                coeffs[i, skip : skip + high - low, :] = ref[low:high, :]


def chunks(start, count):
    out = list(range(start, start + count - 7, 8))
    if count % 8:
        out.append(start + count - 8)
    return out


def smooth_rows(coeffs, field, start, index):
    d = coeffs[0, start : start + 8, :]
    vy = coeffs[2, start : start + 8, :]
    return (
        (1.0 - 2.0 * d) * field[index, start : start + 8, :]
        + (d + vy) * field[index, start - 1 : start + 7, :]
        + (d - vy) * field[index, start + 1 : start + 9, :]
    )


def shift_of(d, dz):
    a = 1.0 - 2.0 * d
    return 1.0 - a * a + 2.0 * dz


def first_kernel(gathered, coeffs, start_field, smoothed):
    slots = slots_at(THERE, position()[4])
    for r in chunks(0, WIDE):
        values = []
        for n in range(NT):
            base = WIDE * (n % 4) + r
            value = gathered[slots[n // 4], base : base + 8, :]
            values.append(value * math.exp(n * LOG_G) if n else value)
        spec = real_fft(values)
        h = shift_of(coeffs[0, r : r + 8, :], coeffs[3, r : r + 8, :])
        for pair in range(16):
            a, b = (spec[0][0], spec[16][0]) if pair == 0 else spec[pair]
            ya, yb = apply_inverse(pair, inverses(pair, h), a, b)
            start_field[2 * pair, r : r + 8, :] = ya
            start_field[2 * pair + 1, r : r + 8, :] = yb
    for r in chunks(1, SMOOTH):
        for f in range(NT):
            base = SMOOTH * f + r - 1
            smoothed[base : base + 8, :] = smooth_rows(coeffs, start_field, r, f)


def sweep_rows(coeffs, field, near, far, start, bases, keep):
    rows = slice(start, start + 8)
    d, vx, vy, dz = (coeffs[i, rows, :] for i in range(4))
    a = 1.0 - 2.0 * d
    up, down = a * (d + vy), a * (d - vy)
    sign = (2 * position()[3] - 1).astype(jnp.float32)
    beside, across = d + sign * vx, d - sign * vx
    h = shift_of(d, dz)
    lane = lax.broadcasted_iota(jnp.int32, (8, 128), 1)
    below = jnp.where(lane == 0, 0.0, dz)
    above = jnp.where(lane == 127, 0.0, dz)
    for pair in range(16):
        both = []
        for f in (2 * pair, 2 * pair + 1):
            center = field[f, rows, :]
            base = bases(f)
            both.append(
                up * field[f, start - 1 : start + 7, :]
                + down * field[f, start + 1 : start + 9, :]
                + beside * near[base : base + 8, :]
                + across * far[base : base + 8, :]
                + below * pltpu.roll(center, 1, 1)
                + above * pltpu.roll(center, 127, 1)
            )
        keep(pair, *apply_inverse(pair, inverses(pair, h), *both))


def second_kernel(coeffs, start_field, near, far, next_field, smoothed):
    for r in chunks(1, SMOOTH):

        def keep(pair, a, b):
            for f, value in ((2 * pair, a), (2 * pair + 1, b)):
                next_field[f, r : r + 8, :] = start_field[f, r : r + 8, :] + value

        sweep_rows(coeffs, start_field, near, far, r, lambda f: SMOOTH * f + r - 1, keep)
    for r in chunks(2, ROWS):
        for f in range(NT):
            base = ROWS * f + r - 2
            smoothed[base : base + 8, :] = smooth_rows(coeffs, next_field, r, f)


def third_kernel(coeffs, start_field, next_field, near, far, blocks):
    slots = slots_at(BACK, position()[4])
    for r in chunks(2, ROWS):
        spec = [None] * 17

        def keep(pair, a, b):
            a = start_field[2 * pair, r : r + 8, :] + a
            b = start_field[2 * pair + 1, r : r + 8, :] + b
            if pair == 0:
                spec[0], spec[16] = (a, None), (b, None)
            else:
                spec[pair] = (a, b)

        sweep_rows(coeffs, next_field, near, far, r, lambda f: ROWS * f + r - 2, keep)
        for n, value in enumerate(real_ifft(spec)):
            base = ROWS * (n % 4) + r - 2
            blocks[slots[n // 4], base : base + 8, :] = value * (math.exp(-n * LOG_G) / NT)


def unpack_kernel(gathered, out, sems):
    _, _, odd_x, _, z = position()
    slots = slots_at(BACK, z)
    copies = []
    for half in range(2):
        tracer = odd_x if half == 0 else 1 - odd_x
        for part in range(4):
            block = 2 * part + half
            target = out.at[:, tracer, pl.ds(ROWS * part, ROWS), :]
            copies.append(pltpu.make_async_copy(gathered.at[slots[block]], target, sems.at[block]))
    for copy in copies:
        copy.start()
    for copy in copies:
        copy.wait()


def f32(*shape):
    return jax.ShapeDtypeStruct(shape, jnp.float32)


def call(kernel, outs, inputs=1, far_in=False, far_out=False, scratch=()):
    vmem = pl.BlockSpec(memory_space=pltpu.VMEM)
    hbm = pl.BlockSpec(memory_space=pltpu.HBM)
    out_spec = hbm if far_out else vmem
    return pl.pallas_call(
        kernel,
        out_shape=outs,
        in_specs=[hbm if far_in else vmem] * inputs,
        out_specs=(out_spec,) * len(outs) if isinstance(outs, tuple) else out_spec,
        scratch_shapes=list(scratch),
        compiler_params=pltpu.CompilerParams(vmem_limit_bytes=VMEM),
    )


def shards(forcing, init_state, prev_last, diff_h, vel_x, vel_y, diff_z):
    near, far = swaps()
    axes = ("tm", "space")
    operands = (
        forcing.reshape(4, 2, 128, 128),
        init_state.reshape(2, 128, 128),
        prev_last.reshape(2, 128, 128),
        *(c.reshape(128, 128) for c in (diff_h, vel_x, vel_y, diff_z)),
    )
    order = (0, 3, 4, 5, 6, 1, 2)
    scratch = [pltpu.VMEM(operands[i].shape, jnp.float32) for i in order] + [pltpu.SemaphoreType.DMA((10,))]
    blocks, coeffs = call(pack_kernel, (f32(8, 4 * WIDE, 128), f32(4, 40, 128)), 7, far_in=True, scratch=scratch)(
        *(pltpu.with_memory_space_constraint(a, pltpu.HBM) for a in operands)
    )
    gathered = exchange(THERE, blocks)
    start_field, smoothed = call(first_kernel, (f32(NT, 40, 128), f32(NT * SMOOTH, 128)), 2)(gathered, coeffs)
    across = lax.ppermute(smoothed, axes, far)
    beside = lax.ppermute(smoothed, axes, near)
    next_field, smoothed = call(second_kernel, (f32(NT, 40, 128), f32(NT * ROWS, 128)), 4)(
        coeffs, start_field, beside, across
    )
    across = lax.ppermute(smoothed, axes, far)
    beside = lax.ppermute(smoothed, axes, near)
    blocks = call(third_kernel, f32(8, 4 * ROWS, 128), 5)(coeffs, start_field, next_field, beside, across)
    gathered = exchange(BACK, blocks).reshape(8, 4, ROWS, 128)
    out = call(unpack_kernel, f32(4, 2, 128, 128), 1, far_out=True, scratch=[pltpu.SemaphoreType.DMA((8,))])(gathered)
    return out.reshape(forcing.shape)


def solution(mesh):
    return jax.shard_map(
        shards,
        mesh=mesh,
        in_specs=(
            P("tm", None, "space", None, None),
            P(None, "space", None, None),
            P(None, "space", None, None),
            P("space", None, None),
            P("space", None, None),
            P("space", None, None),
            P("space", None, None),
        ),
        out_specs=P("tm", None, "space", None, None),
        check_vma=False,
    )
```

```python
import math

import jax
import jax.numpy as jnp
from jax import lax
from jax.experimental import pallas as pl
from jax.experimental.pallas import tpu as pltpu
from jax.sharding import PartitionSpec as P

CORNER = 0.5
NT = 32
LOG_G = math.log(CORNER) / NT
G = math.exp(LOG_G)
ROWS = 32
WIDE = ROWS + 4
SMOOTH = ROWS + 2
VMEM = 24 * 1024 * 1024

CHIPS_X, CHIPS_Y, CHIPS_Z, CORES = 4, 4, 16, 2


def flat_index(x, y, z, core):
    half = CHIPS_Z // 2
    return (y * 2 + z // half) * (CHIPS_X * half * CORES) + (x * half + z % half) * CORES + core


def position():
    group, place = lax.axis_index("tm"), lax.axis_index("space")
    return group >> 1, group & 1, (place >> 4) & 1, place & 1, (place >> 1) & 7


THERE = (16449171, 477046, 13642849, 7670213, 9222927, 4329496, 11130092, 4187066)
BACK = (12686257, 15687935, 4709462, 3586597, 10243739, 11053032, 7502090, 1639748)


def slots_at(places, z):
    return [(place >> (3 * z)) & 7 for place in places]


def exchange(places, blocks):
    half = CHIPS_Z // 2
    groups = []
    for x in range(CHIPS_X):
        for z in range(half):
            slots = slots_at(places, z)
            for core in range(CORES):
                members = [0] * 8
                for group, slot in enumerate(slots):
                    members[slot] = flat_index(x, group // 2, z + half * (group % 2), core)
                groups.append(members)
    return lax.all_to_all(blocks, ("tm", "space"), 0, 0, axis_index_groups=groups)


def swaps():
    near, far = [], []
    half = CHIPS_Z // 2
    for x in range(CHIPS_X):
        for y in range(CHIPS_Y):
            for z in range(CHIPS_Z):
                here, mate = flat_index(x, y, z, 0), flat_index(x, y, z, 1)
                near += [(here, mate), (mate, here)]
                step = x + 1 if z % half == half - 1 else x
                if step < CHIPS_X:
                    after = flat_index(step, y, (z + 1) % CHIPS_Z, 0)
                    far += [(mate, after), (after, mate)]
    return near, far


def real_fft(values):
    n = len(values)
    if n == 1:
        return [(values[0], None)]
    if n == 2:
        return [(values[0] + values[1], None), (values[0] - values[1], None)]
    even, odd = real_fft(values[0::2]), real_fft(values[1::2])
    out = [None] * (n // 2 + 1)
    out[0] = (even[0][0] + odd[0][0], None)
    out[n // 2] = (even[0][0] - odd[0][0], None)
    for k in range(1, n // 4):
        c, s = math.cos(2 * math.pi * k / n), math.sin(2 * math.pi * k / n)
        er, ei = even[k]
        orr, oi = odd[k]
        tr = c * orr + s * oi
        ti = c * oi - s * orr
        out[k] = (er + tr, ei + ti)
        out[n // 2 - k] = (er - tr, ti - ei)
    out[n // 4] = (even[n // 4][0], -odd[n // 4][0])
    return out


def real_ifft(spec):
    n = 2 * (len(spec) - 1)
    if n == 2:
        return [spec[0][0] + spec[1][0], spec[0][0] - spec[1][0]]
    even, odd = [None] * (n // 4 + 1), [None] * (n // 4 + 1)
    even[0] = (spec[0][0] + spec[n // 2][0], None)
    odd[0] = (spec[0][0] - spec[n // 2][0], None)
    for k in range(1, n // 4):
        c, s = math.cos(2 * math.pi * k / n), math.sin(2 * math.pi * k / n)
        ar, ai = spec[k]
        br, bi = spec[n // 2 - k]
        even[k] = (ar + br, ai - bi)
        dr, di = ar - br, ai + bi
        odd[k] = (c * dr - s * di, c * di + s * dr)
    even[n // 4] = (2.0 * spec[n // 4][0], None)
    odd[n // 4] = (-2.0 * spec[n // 4][1], None)
    first, second = real_ifft(even), real_ifft(odd)
    out = [None] * n
    out[0::2], out[1::2] = first, second
    return out


def inverses(pair, h):
    if pair == 0:
        return 1.0 / (h + (1.0 - G)), 1.0 / (h + (1.0 + G))
    theta = 2.0 * math.pi * pair / NT
    real = h + (1.0 - G * math.cos(theta))
    imag = G * math.sin(theta)
    scale = 1.0 / (real * real + imag * imag)
    return real * scale, imag * scale


def apply_inverse(pair, inv, first, second):
    if pair == 0:
        return first * inv[0], second * inv[1]
    return first * inv[0] + second * inv[1], second * inv[0] - first * inv[1]


def window(part):
    low, high = max(ROWS * part - 2, 0), min(ROWS * part + ROWS + 2, 128)
    return low, high, low - (ROWS * part - 2)


def pack_kernel(forcing, init, prev, *refs):
    sources, (blocks, coeffs), held, sems = refs[:4], refs[4:6], refs[6:13], refs[13]
    quarter, own_half, odd_x, _, z = position()
    slots = slots_at(THERE, z)
    steps, values, firsts = held[0], held[1:5], held[5:7]
    loads = [pltpu.make_async_copy(forcing.at[step], steps.at[step], sems.at[step]) for step in range(4)]
    others = [pltpu.make_async_copy(source, values[i], sems.at[4 + i]) for i, source in enumerate(sources)]
    holds_first = jnp.logical_and(quarter == 0, own_half == 0)
    for copy in loads + others:
        copy.start()

    @pl.when(holds_first)
    def _():
        pair = [pltpu.make_async_copy(a, firsts[i], sems.at[8 + i]) for i, a in enumerate((init, prev))]
        for copy in pair:
            copy.start()
        for copy in pair:
            copy.wait()

    loads[0].wait()

    @pl.when(holds_first)
    def _():
        steps[0] += firsts[0][...] - CORNER * firsts[1][...]

    for step in range(4):
        if step:
            loads[step].wait()
        for half in range(2):
            tracer = odd_x if half == 0 else 1 - odd_x
            for part in range(4):
                low, high, skip = window(part)
                rest = WIDE - skip - (high - low)
                dest, base = slots[2 * part + half], WIDE * step
                blocks[dest, base + skip : base + skip + high - low, :] = steps[step, tracer, low:high, :]
                if skip:
                    blocks[dest, base : base + skip, :] = jnp.zeros((skip, 128), jnp.float32)
                if rest:
                    blocks[dest, base + WIDE - rest : base + WIDE, :] = jnp.zeros((rest, 128), jnp.float32)
    for copy in others:
        copy.wait()
    for part in range(4):

        @pl.when(quarter == part)
        def _():
            low, high, skip = window(part)
            if part in (0, 3):
                coeffs[...] = jnp.zeros(coeffs.shape, jnp.float32)
            for i, ref in enumerate(values):
                coeffs[i, skip : skip + high - low, :] = ref[low:high, :]


def chunks(start, count):
    out = list(range(start, start + count - 7, 8))
    if count % 8:
        out.append(start + count - 8)
    return out


def smooth_rows(coeffs, field, start, index):
    d = coeffs[0, start : start + 8, :]
    vy = coeffs[2, start : start + 8, :]
    return (
        (1.0 - 2.0 * d) * field[index, start : start + 8, :]
        + (d + vy) * field[index, start - 1 : start + 7, :]
        + (d - vy) * field[index, start + 1 : start + 9, :]
    )


def shift_of(d, dz):
    a = 1.0 - 2.0 * d
    return 1.0 - a * a + 2.0 * dz


def first_kernel(gathered, coeffs, start_field, smoothed):
    slots = slots_at(THERE, position()[4])
    for r in chunks(0, WIDE):
        values = []
        for n in range(NT):
            base = WIDE * (n % 4) + r
            value = gathered[slots[n // 4], base : base + 8, :]
            values.append(value * math.exp(n * LOG_G) if n else value)
        spec = real_fft(values)
        h = shift_of(coeffs[0, r : r + 8, :], coeffs[3, r : r + 8, :])
        for pair in range(16):
            a, b = (spec[0][0], spec[16][0]) if pair == 0 else spec[pair]
            ya, yb = apply_inverse(pair, inverses(pair, h), a, b)
            start_field[2 * pair, r : r + 8, :] = ya
            start_field[2 * pair + 1, r : r + 8, :] = yb
    for r in chunks(1, SMOOTH):
        for f in range(NT):
            base = SMOOTH * f + r - 1
            smoothed[base : base + 8, :] = smooth_rows(coeffs, start_field, r, f)


def sweep_rows(coeffs, field, near, far, start, bases, keep):
    rows = slice(start, start + 8)
    d, vx, vy, dz = (coeffs[i, rows, :] for i in range(4))
    a = 1.0 - 2.0 * d
    up, down = a * (d + vy), a * (d - vy)
    sign = (2 * position()[3] - 1).astype(jnp.float32)
    beside, across = d + sign * vx, d - sign * vx
    h = shift_of(d, dz)
    lane = lax.broadcasted_iota(jnp.int32, (8, 128), 1)
    below = jnp.where(lane == 0, 0.0, dz)
    above = jnp.where(lane == 127, 0.0, dz)
    for pair in range(16):
        both = []
        for f in (2 * pair, 2 * pair + 1):
            center = field[f, rows, :]
            base = bases(f)
            both.append(
                up * field[f, start - 1 : start + 7, :]
                + down * field[f, start + 1 : start + 9, :]
                + beside * near[base : base + 8, :]
                + across * far[base : base + 8, :]
                + below * pltpu.roll(center, 1, 1)
                + above * pltpu.roll(center, 127, 1)
            )
        keep(pair, *apply_inverse(pair, inverses(pair, h), *both))


def second_kernel(coeffs, start_field, near, far, next_field, smoothed):
    for r in chunks(1, SMOOTH):

        def keep(pair, a, b):
            for f, value in ((2 * pair, a), (2 * pair + 1, b)):
                next_field[f, r : r + 8, :] = start_field[f, r : r + 8, :] + value

        sweep_rows(coeffs, start_field, near, far, r, lambda f: SMOOTH * f + r - 1, keep)
    for r in chunks(2, ROWS):
        for f in range(NT):
            base = ROWS * f + r - 2
            smoothed[base : base + 8, :] = smooth_rows(coeffs, next_field, r, f)


def third_kernel(coeffs, start_field, next_field, near, far, blocks):
    slots = slots_at(BACK, position()[4])
    for r in chunks(2, ROWS):
        spec = [None] * 17

        def keep(pair, a, b):
            a = start_field[2 * pair, r : r + 8, :] + a
            b = start_field[2 * pair + 1, r : r + 8, :] + b
            if pair == 0:
                spec[0], spec[16] = (a, None), (b, None)
            else:
                spec[pair] = (a, b)

        sweep_rows(coeffs, next_field, near, far, r, lambda f: ROWS * f + r - 2, keep)
        for n, value in enumerate(real_ifft(spec)):
            base = ROWS * (n % 4) + r - 2
            blocks[slots[n // 4], base : base + 8, :] = value * (math.exp(-n * LOG_G) / NT)


def unpack_kernel(gathered, out, sems):
    _, _, odd_x, _, z = position()
    slots = slots_at(BACK, z)
    copies = []
    for half in range(2):
        tracer = odd_x if half == 0 else 1 - odd_x
        for part in range(4):
            block = 2 * part + half
            target = out.at[:, tracer, pl.ds(ROWS * part, ROWS), :]
            copies.append(pltpu.make_async_copy(gathered.at[slots[block]], target, sems.at[block]))
    for copy in copies:
        copy.start()
    for copy in copies:
        copy.wait()


def f32(*shape):
    return jax.ShapeDtypeStruct(shape, jnp.float32)


def call(kernel, outs, inputs=1, far_in=False, far_out=False, scratch=()):
    vmem = pl.BlockSpec(memory_space=pltpu.VMEM)
    hbm = pl.BlockSpec(memory_space=pltpu.HBM)
    out_spec = hbm if far_out else vmem
    return pl.pallas_call(
        kernel,
        out_shape=outs,
        in_specs=[hbm if far_in else vmem] * inputs,
        out_specs=(out_spec,) * len(outs) if isinstance(outs, tuple) else out_spec,
        scratch_shapes=list(scratch),
        compiler_params=pltpu.CompilerParams(vmem_limit_bytes=VMEM),
    )


def shards(forcing, init_state, prev_last, diff_h, vel_x, vel_y, diff_z):
    near, far = swaps()
    axes = ("tm", "space")
    operands = (
        forcing.reshape(4, 2, 128, 128),
        init_state.reshape(2, 128, 128),
        prev_last.reshape(2, 128, 128),
        *(c.reshape(128, 128) for c in (diff_h, vel_x, vel_y, diff_z)),
    )
    order = (0, 3, 4, 5, 6, 1, 2)
    scratch = [pltpu.VMEM(operands[i].shape, jnp.float32) for i in order] + [pltpu.SemaphoreType.DMA((10,))]
    blocks, coeffs = call(pack_kernel, (f32(8, 4 * WIDE, 128), f32(4, 40, 128)), 7, far_in=True, scratch=scratch)(
        *(pltpu.with_memory_space_constraint(a, pltpu.HBM) for a in operands)
    )
    gathered = exchange(THERE, blocks)
    start_field, smoothed = call(first_kernel, (f32(NT, 40, 128), f32(NT * SMOOTH, 128)), 2)(gathered, coeffs)
    across = lax.ppermute(smoothed, axes, far)
    beside = lax.ppermute(smoothed, axes, near)
    next_field, smoothed = call(second_kernel, (f32(NT, 40, 128), f32(NT * ROWS, 128)), 4)(
        coeffs, start_field, beside, across
    )
    across = lax.ppermute(smoothed, axes, far)
    beside = lax.ppermute(smoothed, axes, near)
    blocks = call(third_kernel, f32(8, 4 * ROWS, 128), 5)(coeffs, start_field, next_field, beside, across)
    gathered = exchange(BACK, blocks).reshape(8, 4, ROWS, 128)
    out = call(unpack_kernel, f32(4, 2, 128, 128), 1, far_out=True, scratch=[pltpu.SemaphoreType.DMA((8,))])(gathered)
    return out.reshape(forcing.shape)


def solution(mesh):
    return jax.shard_map(
        shards,
        mesh=mesh,
        in_specs=(
            P("tm", None, "space", None, None),
            P(None, "space", None, None),
            P(None, "space", None, None),
            P("space", None, None),
            P("space", None, None),
            P("space", None, None),
            P("space", None, None),
        ),
        out_specs=P("tm", None, "space", None, None),
        check_vma=False,
    )
```

```python
import math

import jax
import jax.numpy as jnp
from jax import lax
from jax.experimental import pallas as pl
from jax.experimental.pallas import tpu as pltpu
from jax.sharding import PartitionSpec as P

CORNER = 0.5
NT = 32
LOG_G = math.log(CORNER) / NT
G = math.exp(LOG_G)
ROWS = 32
WIDE = ROWS + 4
SMOOTH = ROWS + 2
VMEM = 24 * 1024 * 1024

CHIPS_X, CHIPS_Y, CHIPS_Z, CORES = 4, 4, 16, 2


def flat_index(x, y, z, core):
    half = CHIPS_Z // 2
    return (y * 2 + z // half) * (CHIPS_X * half * CORES) + (x * half + z % half) * CORES + core


def position():
    group, place = lax.axis_index("tm"), lax.axis_index("space")
    return group >> 1, group & 1, (place >> 4) & 1, place & 1, (place >> 1) & 7


THERE = (16449171, 477046, 13642849, 7670213, 9222927, 4329496, 11130092, 4187066)
BACK = (12686257, 15687935, 4709462, 3586597, 10243739, 11053032, 7502090, 1639748)


def slots_at(places, z):
    return [(place >> (3 * z)) & 7 for place in places]


def exchange(places, blocks):
    half = CHIPS_Z // 2
    groups = []
    for x in range(CHIPS_X):
        for z in range(half):
            slots = slots_at(places, z)
            for core in range(CORES):
                members = [0] * 8
                for group, slot in enumerate(slots):
                    members[slot] = flat_index(x, group // 2, z + half * (group % 2), core)
                groups.append(members)
    return lax.all_to_all(blocks, ("tm", "space"), 0, 0, axis_index_groups=groups)


def swaps():
    near, far = [], []
    half = CHIPS_Z // 2
    for x in range(CHIPS_X):
        for y in range(CHIPS_Y):
            for z in range(CHIPS_Z):
                here, mate = flat_index(x, y, z, 0), flat_index(x, y, z, 1)
                near += [(here, mate), (mate, here)]
                step = x + 1 if z % half == half - 1 else x
                if step < CHIPS_X:
                    after = flat_index(step, y, (z + 1) % CHIPS_Z, 0)
                    far += [(mate, after), (after, mate)]
    return near, far


def real_fft(values):
    n = len(values)
    if n == 1:
        return [(values[0], None)]
    if n == 2:
        return [(values[0] + values[1], None), (values[0] - values[1], None)]
    even, odd = real_fft(values[0::2]), real_fft(values[1::2])
    out = [None] * (n // 2 + 1)
    out[0] = (even[0][0] + odd[0][0], None)
    out[n // 2] = (even[0][0] - odd[0][0], None)
    for k in range(1, n // 4):
        c, s = math.cos(2 * math.pi * k / n), math.sin(2 * math.pi * k / n)
        er, ei = even[k]
        orr, oi = odd[k]
        tr = c * orr + s * oi
        ti = c * oi - s * orr
        out[k] = (er + tr, ei + ti)
        out[n // 2 - k] = (er - tr, ti - ei)
    out[n // 4] = (even[n // 4][0], -odd[n // 4][0])
    return out


def real_ifft(spec):
    n = 2 * (len(spec) - 1)
    if n == 2:
        return [spec[0][0] + spec[1][0], spec[0][0] - spec[1][0]]
    even, odd = [None] * (n // 4 + 1), [None] * (n // 4 + 1)
    even[0] = (spec[0][0] + spec[n // 2][0], None)
    odd[0] = (spec[0][0] - spec[n // 2][0], None)
    for k in range(1, n // 4):
        c, s = math.cos(2 * math.pi * k / n), math.sin(2 * math.pi * k / n)
        ar, ai = spec[k]
        br, bi = spec[n // 2 - k]
        even[k] = (ar + br, ai - bi)
        dr, di = ar - br, ai + bi
        odd[k] = (c * dr - s * di, c * di + s * dr)
    even[n // 4] = (2.0 * spec[n // 4][0], None)
    odd[n // 4] = (-2.0 * spec[n // 4][1], None)
    first, second = real_ifft(even), real_ifft(odd)
    out = [None] * n
    out[0::2], out[1::2] = first, second
    return out


def inverses(pair, h):
    if pair == 0:
        return 1.0 / (h + (1.0 - G)), 1.0 / (h + (1.0 + G))
    theta = 2.0 * math.pi * pair / NT
    real = h + (1.0 - G * math.cos(theta))
    imag = G * math.sin(theta)
    scale = 1.0 / (real * real + imag * imag)
    return real * scale, imag * scale


def apply_inverse(pair, inv, first, second):
    if pair == 0:
        return first * inv[0], second * inv[1]
    return first * inv[0] + second * inv[1], second * inv[0] - first * inv[1]


def window(part):
    low, high = max(ROWS * part - 2, 0), min(ROWS * part + ROWS + 2, 128)
    return low, high, low - (ROWS * part - 2)


def pack_kernel(forcing, init, prev, *refs):
    sources, (blocks, coeffs), held, sems = refs[:4], refs[4:6], refs[6:13], refs[13]
    quarter, own_half, odd_x, _, z = position()
    slots = slots_at(THERE, z)
    steps, values, firsts = held[0], held[1:5], held[5:7]
    loads = [pltpu.make_async_copy(forcing.at[step], steps.at[step], sems.at[step]) for step in range(4)]
    others = [pltpu.make_async_copy(source, values[i], sems.at[4 + i]) for i, source in enumerate(sources)]
    holds_first = jnp.logical_and(quarter == 0, own_half == 0)
    for copy in loads[1:] + loads[:1] + others:
        copy.start()

    states = [pltpu.make_async_copy(a, firsts[i], sems.at[8 + i]) for i, a in enumerate((init, prev))]

    @pl.when(holds_first)
    def _():
        for copy in states:
            copy.start()

    for step in (1, 2, 3, 0):
        loads[step].wait()
        if step == 0:

            @pl.when(holds_first)
            def _():
                for copy in states:
                    copy.wait()
                steps[0] += firsts[0][...] - CORNER * firsts[1][...]

        for half in range(2):
            tracer = odd_x if half == 0 else 1 - odd_x
            for part in range(4):
                low, high, skip = window(part)
                rest = WIDE - skip - (high - low)
                dest, base = slots[2 * part + half], WIDE * step
                blocks[dest, base + skip : base + skip + high - low, :] = steps[step, tracer, low:high, :]
                if skip:
                    blocks[dest, base : base + skip, :] = jnp.zeros((skip, 128), jnp.float32)
                if rest:
                    blocks[dest, base + WIDE - rest : base + WIDE, :] = jnp.zeros((rest, 128), jnp.float32)
    for copy in others:
        copy.wait()
    for part in range(4):

        @pl.when(quarter == part)
        def _():
            low, high, skip = window(part)
            if part in (0, 3):
                coeffs[...] = jnp.zeros(coeffs.shape, jnp.float32)
            for i, ref in enumerate(values):
                coeffs[i, skip : skip + high - low, :] = ref[low:high, :]


def chunks(start, count):
    out = list(range(start, start + count - 7, 8))
    if count % 8:
        out.append(start + count - 8)
    return out


def smooth_rows(coeffs, field, start, index):
    d = coeffs[0, start : start + 8, :]
    vy = coeffs[2, start : start + 8, :]
    return (
        (1.0 - 2.0 * d) * field[index, start : start + 8, :]
        + (d + vy) * field[index, start - 1 : start + 7, :]
        + (d - vy) * field[index, start + 1 : start + 9, :]
    )


def shift_of(d, dz):
    a = 1.0 - 2.0 * d
    return 1.0 - a * a + 2.0 * dz


def first_kernel(gathered, coeffs, start_field, smoothed):
    slots = slots_at(THERE, position()[4])
    for r in chunks(0, WIDE):
        values = []
        for n in range(NT):
            base = WIDE * (n % 4) + r
            value = gathered[slots[n // 4], base : base + 8, :]
            values.append(value * math.exp(n * LOG_G) if n else value)
        spec = real_fft(values)
        h = shift_of(coeffs[0, r : r + 8, :], coeffs[3, r : r + 8, :])
        for pair in range(16):
            a, b = (spec[0][0], spec[16][0]) if pair == 0 else spec[pair]
            ya, yb = apply_inverse(pair, inverses(pair, h), a, b)
            start_field[2 * pair, r : r + 8, :] = ya
            start_field[2 * pair + 1, r : r + 8, :] = yb
    for r in chunks(1, SMOOTH):
        for f in range(NT):
            base = SMOOTH * f + r - 1
            smoothed[base : base + 8, :] = smooth_rows(coeffs, start_field, r, f)


def sweep_rows(coeffs, field, near, far, start, bases, keep):
    rows = slice(start, start + 8)
    d, vx, vy, dz = (coeffs[i, rows, :] for i in range(4))
    a = 1.0 - 2.0 * d
    up, down = a * (d + vy), a * (d - vy)
    sign = (2 * position()[3] - 1).astype(jnp.float32)
    beside, across = d + sign * vx, d - sign * vx
    h = shift_of(d, dz)
    lane = lax.broadcasted_iota(jnp.int32, (8, 128), 1)
    below = jnp.where(lane == 0, 0.0, dz)
    above = jnp.where(lane == 127, 0.0, dz)
    for pair in range(16):
        both = []
        for f in (2 * pair, 2 * pair + 1):
            center = field[f, rows, :]
            base = bases(f)
            both.append(
                up * field[f, start - 1 : start + 7, :]
                + down * field[f, start + 1 : start + 9, :]
                + beside * near[base : base + 8, :]
                + across * far[base : base + 8, :]
                + below * pltpu.roll(center, 1, 1)
                + above * pltpu.roll(center, 127, 1)
            )
        keep(pair, *apply_inverse(pair, inverses(pair, h), *both))


def second_kernel(coeffs, start_field, near, far, next_field, smoothed):
    for r in chunks(1, SMOOTH):

        def keep(pair, a, b):
            for f, value in ((2 * pair, a), (2 * pair + 1, b)):
                next_field[f, r : r + 8, :] = start_field[f, r : r + 8, :] + value

        sweep_rows(coeffs, start_field, near, far, r, lambda f: SMOOTH * f + r - 1, keep)
    for r in chunks(2, ROWS):
        for f in range(NT):
            base = ROWS * f + r - 2
            smoothed[base : base + 8, :] = smooth_rows(coeffs, next_field, r, f)


def third_kernel(coeffs, start_field, next_field, near, far, blocks):
    slots = slots_at(BACK, position()[4])
    for r in chunks(2, ROWS):
        spec = [None] * 17

        def keep(pair, a, b):
            a = start_field[2 * pair, r : r + 8, :] + a
            b = start_field[2 * pair + 1, r : r + 8, :] + b
            if pair == 0:
                spec[0], spec[16] = (a, None), (b, None)
            else:
                spec[pair] = (a, b)

        sweep_rows(coeffs, next_field, near, far, r, lambda f: ROWS * f + r - 2, keep)
        for n, value in enumerate(real_ifft(spec)):
            base = ROWS * (n % 4) + r - 2
            blocks[slots[n // 4], base : base + 8, :] = value * (math.exp(-n * LOG_G) / NT)


def unpack_kernel(gathered, out, sems):
    _, _, odd_x, _, z = position()
    slots = slots_at(BACK, z)
    copies = []
    for half in range(2):
        tracer = odd_x if half == 0 else 1 - odd_x
        for part in range(4):
            block = 2 * part + half
            target = out.at[:, tracer, pl.ds(ROWS * part, ROWS), :]
            copies.append(pltpu.make_async_copy(gathered.at[slots[block]], target, sems.at[block]))
    for copy in copies:
        copy.start()
    for copy in copies:
        copy.wait()


def f32(*shape):
    return jax.ShapeDtypeStruct(shape, jnp.float32)


def call(kernel, outs, inputs=1, far_in=False, far_out=False, scratch=()):
    vmem = pl.BlockSpec(memory_space=pltpu.VMEM)
    hbm = pl.BlockSpec(memory_space=pltpu.HBM)
    out_spec = hbm if far_out else vmem
    return pl.pallas_call(
        kernel,
        out_shape=outs,
        in_specs=[hbm if far_in else vmem] * inputs,
        out_specs=(out_spec,) * len(outs) if isinstance(outs, tuple) else out_spec,
        scratch_shapes=list(scratch),
        compiler_params=pltpu.CompilerParams(vmem_limit_bytes=VMEM),
    )


def shards(forcing, init_state, prev_last, diff_h, vel_x, vel_y, diff_z):
    near, far = swaps()
    axes = ("tm", "space")
    operands = (
        forcing.reshape(4, 2, 128, 128),
        init_state.reshape(2, 128, 128),
        prev_last.reshape(2, 128, 128),
        *(c.reshape(128, 128) for c in (diff_h, vel_x, vel_y, diff_z)),
    )
    order = (0, 3, 4, 5, 6, 1, 2)
    scratch = [pltpu.VMEM(operands[i].shape, jnp.float32) for i in order] + [pltpu.SemaphoreType.DMA((10,))]
    blocks, coeffs = call(pack_kernel, (f32(8, 4 * WIDE, 128), f32(4, 40, 128)), 7, far_in=True, scratch=scratch)(
        *(pltpu.with_memory_space_constraint(a, pltpu.HBM) for a in operands)
    )
    gathered = exchange(THERE, blocks)
    start_field, smoothed = call(first_kernel, (f32(NT, 40, 128), f32(NT * SMOOTH, 128)), 2)(gathered, coeffs)
    across = lax.ppermute(smoothed, axes, far)
    beside = lax.ppermute(smoothed, axes, near)
    next_field, smoothed = call(second_kernel, (f32(NT, 40, 128), f32(NT * ROWS, 128)), 4)(
        coeffs, start_field, beside, across
    )
    across = lax.ppermute(smoothed, axes, far)
    beside = lax.ppermute(smoothed, axes, near)
    blocks = call(third_kernel, f32(8, 4 * ROWS, 128), 5)(coeffs, start_field, next_field, beside, across)
    gathered = exchange(BACK, blocks).reshape(8, 4, ROWS, 128)
    out = call(unpack_kernel, f32(4, 2, 128, 128), 1, far_out=True, scratch=[pltpu.SemaphoreType.DMA((8,))])(gathered)
    return out.reshape(forcing.shape)


def solution(mesh):
    return jax.shard_map(
        shards,
        mesh=mesh,
        in_specs=(
            P("tm", None, "space", None, None),
            P(None, "space", None, None),
            P(None, "space", None, None),
            P("space", None, None),
            P("space", None, None),
            P("space", None, None),
            P("space", None, None),
        ),
        out_specs=P("tm", None, "space", None, None),
        check_vma=False,
    )
```
